32 devices in a mesh: ctx: 8 (over y, x, core), exp: 4 (over z).
Axes of the slice: x: 2, y: 2, z: 4, core: 2. Of those that a mesh axis runs over, the one named last changes fastest.
Arguments:
- stream: bfloat16 [1024, 4096], P(('ctx', 'exp')), may hold values from -3 to 3
- queries: bfloat16 [1024, 4096], P('ctx', 'exp'), may hold values from -108 to 108
- attn_keys: bfloat16 [1024, 1024], P('ctx', 'exp'), may hold values from -3 to 3
- attn_values: bfloat16 [1024, 1024], P('ctx', 'exp'), may hold values from -6 to 6
- out_weight: bfloat16 [4096, 4096], P('exp'), may hold values from -0.09375 to 0.09375
- norm_gain: float32 [4096], replicated, may hold values from 0.25 to 1.75
- expert_ids: int32 [1024, 2], P(('ctx', 'exp')), may hold values from 0 to 3, all different within a row; in each aligned block of 32 rows (0 to 31, 32 to 63, ...) at most 32 rows name the same one
- combine: float32 [1024, 2], P(('ctx', 'exp')), may hold values from 0.1 to 0.9
- w_gate: bfloat16 [4, 4096, 14336], P('exp', None, 'ctx'), may hold values from -0.09375 to 0.09375
- w_up: bfloat16 [4, 4096, 14336], P('exp', None, 'ctx'), may hold values from -0.09375 to 0.09375
- w_down: bfloat16 [4, 14336, 4096], P('exp', 'ctx'), may hold values from -0.046875 to 0.046875
Outputs:
- layer_out: bfloat16 [1024, 4096], P(('ctx', 'exp'))
The draws below stay inside these ranges and needn't reach their ends.
Inputs may be any that keep to these rules, and one draw needn't show every extreme that they name: `expert_ids`: taking the rows in aligned blocks of 32 (the rows of one device), no expert is named by more than 32 rows of a block, and in every draw some block names some expert exactly 32 times. The 2 experts of a row differ.
All inputs are finite; a program needn't handle non-finite values.
Results may differ from the reference program's by a relative error of at most 0.015.
Values may be sent and summed in bfloat16 or wider, within the bound.
No kernel may reach another device: no remote copies, remote signals or barrier semaphores. Data moves between devices by JAX's collectives and lax.ppermute only.
A program may use at most 128 MiB of HBM per device.

```python
import math
import jax
import jax.numpy as jnp
import numpy as np
from jax import lax

D = 4096
HEADS = 32
KV_HEADS = 8
HEAD_DIM = 128
FF = 14336
TOP = 2
GROUP = 4
EXPERTS = 4
SEQ = 1024
TOK_ROWS = 32
CAP = 32


def joint_draw(key):
    query_key = jax.random.fold_in(key, 11)
    keys_key = jax.random.fold_in(key, 12)
    keys_field = jnp.clip(jax.random.normal(keys_key, (SEQ, KV_HEADS * HEAD_DIM), jnp.float32), -3.0, 3.0)
    query_field = jnp.clip(2.5 * jax.random.normal(query_key, (SEQ, HEADS * HEAD_DIM), jnp.float32), -10.0, 10.0)
    return (query_field, keys_field)


def draw_queries(key, part):
    return joint_draw(key)[0].astype(jnp.bfloat16)


def draw_attn_keys(key, part):
    return joint_draw(key)[1].astype(jnp.bfloat16)


def level_of(key, shape, split, least, top_value):
    loudness, own = 1.0, jax.random.fold_in(key, 6)
    for dim, parts in split:
        steps = jnp.exp(jax.random.uniform(jax.random.fold_in(own, dim), (parts,), jnp.float32, least / len(split), top_value / len(split)))
        loudness = loudness * jnp.repeat(steps, shape[dim] // parts).reshape([-1 if axis == dim else 1 for axis in range(len(shape))])
    return loudness


def assign_block(rng, own, number, rows, number_of, top, reach, slope):
    order = jax.random.permutation(rng, number_of)
    crowded, ordinary = load_shares(number_of, rows * top, reach, slope, True), load_shares(number_of, rows * top, reach, slope, False)
    places = jnp.arange(number_of)

    def named(tallies, turn):
        used = int((tallies > 0).sum())
        fixed = max(1, used // 4)
        shifted = fixed + (places - fixed + turn * (used - fixed)) % max(1, number_of - fixed)
        return jnp.zeros((number_of,), jnp.int32).at[order[jnp.where(places < fixed, places, shifted)]].set(jnp.asarray(tallies, jnp.int32))

    tallies = jnp.where(number % 4 == 0, named(crowded, number // 4), named(ordinary, number - number // 4 - 1))
    mixed = jax.random.permutation(jax.random.fold_in(own, 3), number_of)
    giver, sink = mixed[0:number_of // 2 * 2:2], mixed[1:number_of // 2 * 2:2]
    slack = jnp.minimum(tallies[giver] - 1, reach - tallies[sink]) // 2
    slack = jnp.where((giver == order[0]) | (sink == order[0]) | (tallies[sink] == 0), 0, jnp.maximum(slack, 0))
    shifted = jax.random.randint(jax.random.fold_in(own, 4), (number_of // 2,), 0, 1 << 20) % (slack + 1)
    tallies = tallies.at[giver].add(-shifted).at[sink].add(shifted)
    items = jnp.searchsorted(jnp.cumsum(tallies), jnp.arange(rows * top), side="right").astype(jnp.int32)
    grid = items.reshape(top, rows).T
    grid = grid[jax.random.permutation(jax.random.fold_in(own, 1), rows)]
    turn = jax.random.randint(jax.random.fold_in(own, 2), (rows, 1), 0, top)
    return jnp.take_along_axis(grid, (jnp.arange(top)[None, :] + turn) % top, axis=1)


def load_shares(count, total, reach, slope, full):
    portions = [(1 << 20) // math.isqrt(standing ** slope) + 1 for standing in range(1, count + 1)]
    largest = reach if full else min(reach, max(-(-total // count), total * portions[0] // sum(portions)))
    least = 1 if total - largest >= count - 1 else 0
    given, spare = [largest] + [least] * (count - 1), total - largest - least * (count - 1)
    while spare > 0:
        movable = [i for i in range(1, count) if given[i] < largest] or [i for i in range(1, count) if given[i] < reach]
        mass, remaining = sum([portions[i] for i in movable]), spare
        for i in movable:
            extra = min(reach - given[i], max(1, remaining * portions[i] // mass), spare)
            given[i] = given[i] + extra
            spare = spare - extra
    return np.array(given)


def noise(stream_key, dims, spread, bound, shards=(), held_as=jnp.bfloat16):
    array = spread * jax.random.normal(stream_key, dims, jnp.float32)
    if shards:
        array = array * level_of(stream_key, dims, shards, -0.22, 0.18)
    return jnp.clip(array, -bound, bound).astype(held_as)


def setup_inputs(seed: int = 0) -> dict:
    splits = jax.random.split(jax.random.key(seed), 12)
    stream = noise(splits[0], (SEQ, D), 0.5, 3.0, ((0, 32),))
    queries = draw_queries(jax.random.fold_in(splits[11], 71), 0)
    attn_keys = draw_attn_keys(jax.random.fold_in(splits[11], 71), 0)
    attn_values = noise(splits[3], (SEQ, KV_HEADS * HEAD_DIM), 1.0, 6.0, ((0, 8), (1, 4)))
    out_weight = noise(splits[4], (HEADS * HEAD_DIM, D), (HEADS * HEAD_DIM) ** -0.5, 0.09375, ((0, 4),))
    norm_gain = jnp.clip(1.0 + 0.15 * jax.random.normal(splits[5], (D,), jnp.float32), 0.25, 1.75)
    expert_ids_keys = jax.random.split(jax.random.fold_in(splits[6], 1), SEQ // TOK_ROWS)
    expert_ids_turns = jax.random.permutation(jax.random.fold_in(splits[6], 3), SEQ // TOK_ROWS)
    expert_ids = jax.vmap(lambda own, number: assign_block(jax.random.fold_in(splits[6], 2), own, number, TOK_ROWS, EXPERTS, TOP, CAP, 2))(expert_ids_keys, expert_ids_turns).reshape((SEQ, TOP))
    combine = jnp.clip(0.1 + 0.79999997 * jax.random.uniform(splits[7], (SEQ, TOP), jnp.float32) ** level_of(splits[7], (SEQ, TOP), ((0, 32),), -0.2, 0.2), 0.1, 0.9)
    w_gate = noise(splits[8], (EXPERTS, D, FF), D ** -0.5, 0.09375, ((0, 4), (2, 8)))
    w_up = noise(splits[9], (EXPERTS, D, FF), D ** -0.5, 0.09375, ((0, 4), (2, 8)))
    w_down = noise(splits[10], (EXPERTS, FF, D), FF ** -0.5, 0.046875, ((0, 4), (1, 8)))
    return dict(stream=stream, queries=queries, attn_keys=attn_keys, attn_values=attn_values, out_weight=out_weight, norm_gain=norm_gain, expert_ids=expert_ids, combine=combine, w_gate=w_gate, w_up=w_up, w_down=w_down)


block_rows = 128
neg_big = -1e+30

def head_attention(operands):
    query_group, key_head, value_head = operands
    positions = jnp.arange(SEQ, dtype=jnp.int32)
    allowed = positions[:, None] >= positions[None, :]
    scores = jnp.einsum('tgd,ud->gtu', query_group.astype(jnp.float32), key_head.astype(jnp.float32)) * (1.0 / math.sqrt(HEAD_DIM))
    scores = jnp.where(allowed, scores, neg_big)
    row_max = lax.optimization_barrier(jnp.max(scores, axis=-1, keepdims=True))
    weights = jnp.where(allowed, jnp.exp(scores - row_max), 0.0)
    row_total = lax.optimization_barrier(jnp.sum(weights, axis=-1))
    weight_bf = weights.astype(jnp.bfloat16)
    numerator = jnp.einsum('gtu,ud->tgd', weight_bf.astype(jnp.float32), value_head.astype(jnp.float32))
    return numerator / jnp.transpose(row_total)[..., None]

def reference(stream, queries, attn_keys, attn_values, out_weight, norm_gain, expert_ids, combine, w_gate, w_up, w_down):
    query_heads = jnp.transpose(queries.reshape(SEQ, KV_HEADS, GROUP, HEAD_DIM), (1, 0, 2, 3))
    key_heads = jnp.transpose(attn_keys.reshape(SEQ, KV_HEADS, HEAD_DIM), (1, 0, 2))
    value_heads = jnp.transpose(attn_values.reshape(SEQ, KV_HEADS, HEAD_DIM), (1, 0, 2))
    per_head = lax.map(head_attention, (query_heads, key_heads, value_heads))
    attention = jnp.transpose(per_head, (1, 0, 2, 3)).reshape(SEQ, HEADS * HEAD_DIM).astype(jnp.bfloat16)
    mixed = stream.astype(jnp.float32) + jnp.dot(attention, out_weight, preferred_element_type=jnp.float32)
    mean_square = lax.optimization_barrier(jnp.mean(mixed * mixed, axis=-1, keepdims=True))
    normed = (mixed * lax.rsqrt(mean_square + 1e-05) * norm_gain).astype(jnp.bfloat16)
    total_assign = SEQ * TOP
    flat_ids = expert_ids.reshape(total_assign).astype(jnp.int32)
    token_of = jnp.arange(total_assign, dtype=jnp.int32) // TOP
    onehot = (flat_ids[:, None] == jnp.arange(EXPERTS, dtype=jnp.int32)[None, :]).astype(jnp.int32)
    counts = lax.optimization_barrier(jnp.sum(onehot, axis=0)).astype(jnp.int32)
    slot_rank = lax.optimization_barrier(jnp.sum((jnp.cumsum(onehot, axis=0).astype(jnp.int32) - onehot) * onehot, axis=1)).astype(jnp.int32)
    padded = (counts + block_rows - 1) // block_rows * block_rows
    range_ends = jnp.cumsum(padded).astype(jnp.int32)
    range_begins = range_ends - padded
    dest_row = (range_begins[flat_ids] + slot_rank).astype(jnp.int32)
    n_blocks = (total_assign + block_rows - 1) // block_rows + EXPERTS
    row_token = jnp.zeros((n_blocks * block_rows,), jnp.int32).at[dest_row].set(token_of)
    block_first = jnp.arange(n_blocks, dtype=jnp.int32) * block_rows
    block_expert = jnp.minimum(lax.optimization_barrier(jnp.sum((range_ends[None, :] <= block_first[:, None]).astype(jnp.int32), axis=1)), EXPERTS - 1).astype(jnp.int32)

    def run_block(block_index):
        tokens_here = lax.dynamic_slice_in_dim(row_token, (block_index * block_rows).astype(jnp.int32), block_rows, 0)
        rows_here = jnp.take(normed, tokens_here, axis=0)
        expert_here = block_expert[block_index]
        gate_part = jnp.dot(rows_here, w_gate[expert_here], preferred_element_type=jnp.float32)
        up_part = jnp.dot(rows_here, w_up[expert_here], preferred_element_type=jnp.float32)
        hidden = (jax.nn.silu(gate_part) * up_part).astype(jnp.bfloat16)
        return jnp.dot(hidden, w_down[expert_here], preferred_element_type=jnp.float32).astype(jnp.bfloat16)
    expert_rows = lax.map(run_block, jnp.arange(n_blocks, dtype=jnp.int32)).reshape(n_blocks * block_rows, D)
    expert_out = jnp.take(expert_rows, dest_row, axis=0).reshape(SEQ, TOP, D).astype(jnp.float32)
    layer_out = (mixed + lax.optimization_barrier(jnp.sum(combine[..., None] * expert_out, axis=1))).astype(jnp.bfloat16)
    return layer_out
```

```python
import functools
import math

import jax
import jax.numpy as jnp
from jax import lax
from jax.experimental import pallas as pl
from jax.experimental.pallas import tpu as pltpu
from jax.sharding import PartitionSpec as P

HEAD_DIM = 128
TOP = 2
GROUP = 4
MASKED = -1e30
MIB = 1 << 20


def swap(value, axis, mask):
    count = lax.axis_size(axis)
    return lax.ppermute(value, axis, [(i, i ^ mask) for i in range(count)])


def attend_kernel(
    n_exp, tok_rows, where_ref, q_ref, near_ref, far_ref, weight_hbm, *rest
):
    outs, (att_ref, sorted_ref, weight_ref, weight_sem) = rest[:n_exp], rest[n_exp:]
    fetch = pltpu.make_async_copy(weight_hbm, weight_ref, weight_sem)
    fetch.start()
    span = q_ref.shape[0]
    kv_width = near_ref.shape[1] // 2
    kv_heads = kv_width // HEAD_DIM
    ctx_pos, exp_pos = where_ref[0], where_ref[1]
    n_keys = near_ref.shape[0]
    query_pos = ctx_pos * span + lax.broadcasted_iota(jnp.int32, (span, n_keys), 0)
    column = lax.broadcasted_iota(jnp.int32, (span, n_keys), 1)
    block, within = column // span, column % span
    masks = []
    for core in range(2):
        key_pos = (ctx_pos ^ (2 * block + core)) * span + within
        masks.append(query_pos >= key_pos)
    scale = 1.0 / math.sqrt(HEAD_DIM)
    for g in range(kv_heads):
        keys = slice(g * HEAD_DIM, (g + 1) * HEAD_DIM)
        values = slice(kv_width + g * HEAD_DIM, kv_width + (g + 1) * HEAD_DIM)
        for r in range(GROUP):
            h = g * GROUP + r
            q = q_ref[:, h * HEAD_DIM : (h + 1) * HEAD_DIM]
            scores = []
            for ref, mask in zip((near_ref, far_ref), masks):
                s = lax.dot_general(
                    q, ref[:, keys], (((1,), (1,)), ((), ())), preferred_element_type=jnp.float32
                )
                scores.append(jnp.where(mask, s * scale, MASKED))
            top = jnp.maximum(
                jnp.max(scores[0], axis=1, keepdims=True), jnp.max(scores[1], axis=1, keepdims=True)
            )
            total = jnp.zeros((span, 1), jnp.float32)
            acc = jnp.zeros((span, HEAD_DIM), jnp.float32)
            for ref, s in zip((near_ref, far_ref), scores):
                w = jnp.exp(s - top)
                total = total + jnp.sum(w, axis=1, keepdims=True)
                acc = acc + jnp.dot(
                    w.astype(jnp.bfloat16), ref[:, values], preferred_element_type=jnp.float32
                )
            att_ref[:, h * HEAD_DIM : (h + 1) * HEAD_DIM] = (acc / total).astype(jnp.bfloat16)
    for k in range(n_exp):
        first = pl.multiple_of((exp_pos ^ k) * tok_rows, tok_rows)
        sorted_ref[k * tok_rows : (k + 1) * tok_rows, :] = att_ref[pl.ds(first, tok_rows), :]
    fetch.wait()
    model_dim = weight_ref.shape[1]
    tile = min(1024, model_dim)
    for lo in range(0, model_dim, tile):
        part = jnp.dot(
            sorted_ref[...], weight_ref[:, lo : lo + tile], preferred_element_type=jnp.float32
        ).astype(jnp.bfloat16)
        for k in range(n_exp):
            outs[k][:, lo : lo + tile] = part[k * tok_rows : (k + 1) * tok_rows]


def attend(where, queries, near, far, out_weight, n_exp, tok_rows):
    span = queries.shape[0]
    model_dim = out_weight.shape[1]
    vmem = pl.BlockSpec(memory_space=pltpu.VMEM)
    return pl.pallas_call(
        functools.partial(attend_kernel, n_exp, tok_rows),
        out_shape=[jax.ShapeDtypeStruct((tok_rows, model_dim), jnp.bfloat16)] * n_exp,
        in_specs=[
            pl.BlockSpec(memory_space=pltpu.SMEM),
            vmem,
            vmem,
            vmem,
            pl.BlockSpec(memory_space=pl.ANY),
        ],
        out_specs=[vmem] * n_exp,
        scratch_shapes=[
            pltpu.VMEM(queries.shape, jnp.bfloat16),
            pltpu.VMEM(queries.shape, jnp.bfloat16),
            pltpu.VMEM(out_weight.shape, jnp.bfloat16),
            pltpu.SemaphoreType.DMA(()),
        ],
        compiler_params=pltpu.CompilerParams(vmem_limit_bytes=40 * MIB),
        cost_estimate=pl.CostEstimate(
            flops=8 * 1000 * 1000 * 1000, bytes_accessed=12 * MIB, transcendentals=MIB
        ),
        name="attend",
    )(where, queries, near, far, out_weight)


def norm_kernel(stream_ref, gain_ref, *rest):
    parts, (mixed_ref, normed_ref) = rest[:-2], rest[-2:]
    mixed = stream_ref[...].astype(jnp.float32)
    update = parts[0][...].astype(jnp.float32)
    for part in parts[1:]:
        update = update + part[...].astype(jnp.float32)
    mixed = mixed + update
    mixed_ref[...] = mixed
    mean_square = jnp.mean(mixed * mixed, axis=-1, keepdims=True)
    normed_ref[...] = (mixed * lax.rsqrt(mean_square + 1e-05) * gain_ref[...]).astype(jnp.bfloat16)


def add_and_norm(stream, norm_gain, parts):
    vmem = pl.BlockSpec(memory_space=pltpu.VMEM)
    return pl.pallas_call(
        norm_kernel,
        out_shape=[
            jax.ShapeDtypeStruct(stream.shape, jnp.float32),
            jax.ShapeDtypeStruct(stream.shape, jnp.bfloat16),
        ],
        in_specs=[vmem] * (2 + len(parts)),
        out_specs=[vmem] * 2,
        cost_estimate=pl.CostEstimate(
            flops=6 * stream.size, bytes_accessed=20 * stream.size, transcendentals=0
        ),
        name="add_and_norm",
    )(stream, norm_gain.reshape(1, -1), *parts)


def expert_kernel(n_parts, n_up, *refs):
    parts = refs[:n_parts]
    gate_ref, up_ref, down_ref, keep_ref, send_ref, rows_ref, hidden_ref, sems = refs[n_parts:]
    step = pl.program_id(0)
    rows = parts[0].shape[0]
    tile = gate_ref.shape[2]

    @pl.when(step == 0)
    def _():
        fetches = [
            pltpu.make_async_copy(part, rows_ref.at[pl.ds(i * rows, rows)], sems.at[i])
            for i, part in enumerate(parts)
        ]
        for fetch in fetches:
            fetch.start()
        for fetch in fetches:
            fetch.wait()

    @pl.when(step < n_up)
    def _():
        gate = jnp.dot(rows_ref[...], gate_ref[0], preferred_element_type=jnp.float32)
        up = jnp.dot(rows_ref[...], up_ref[0], preferred_element_type=jnp.float32)
        hidden = gate / (1.0 + jnp.exp(-gate)) * up
        first = pl.multiple_of(step * tile, tile)
        hidden_ref[:, pl.ds(first, tile)] = hidden.astype(jnp.bfloat16)

    @pl.when(step >= n_up)
    def _():
        result = jnp.dot(
            hidden_ref[...], down_ref[0], preferred_element_type=jnp.float32
        ).astype(jnp.bfloat16)
        half = keep_ref.shape[0]
        keep_ref[...] = result[:half]
        send_ref[...] = result[half:]


def expert_rows(parts, w_gate, w_up, w_down):
    n_parts, rows = len(parts), parts[0].shape[0]
    total = n_parts * rows
    _, model_dim, hidden_dim = w_gate.shape
    tile = 256 if hidden_dim % 256 == 0 else 128
    down_tile = 512
    n_up, n_down = hidden_dim // tile, model_dim // down_tile
    half = jax.ShapeDtypeStruct((total // 2, model_dim), jnp.bfloat16)
    up_spec = pl.BlockSpec((1, model_dim, tile), lambda j: (0, 0, jnp.minimum(j, n_up - 1)))
    out_spec = pl.BlockSpec((total // 2, down_tile), lambda j: (0, jnp.maximum(j - n_up, 0)))
    return pl.pallas_call(
        functools.partial(expert_kernel, n_parts, n_up),
        grid=(n_up + n_down,),
        out_shape=[half, half],
        in_specs=[pl.BlockSpec(memory_space=pl.ANY)] * n_parts
        + [
            up_spec,
            up_spec,
            pl.BlockSpec((1, hidden_dim, down_tile), lambda j: (0, 0, jnp.maximum(j - n_up, 0))),
        ],
        out_specs=[out_spec, out_spec],
        scratch_shapes=[
            pltpu.VMEM((total, model_dim), jnp.bfloat16),
            pltpu.VMEM((total, hidden_dim), jnp.bfloat16),
            pltpu.SemaphoreType.DMA((n_parts,)),
        ],
        compiler_params=pltpu.CompilerParams(vmem_limit_bytes=40 * MIB),
        cost_estimate=pl.CostEstimate(
            flops=6 * total * model_dim * hidden_dim,
            bytes_accessed=6 * model_dim * hidden_dim,
            transcendentals=total * hidden_dim,
        ),
        name="expert_rows",
    )(*parts, w_gate, w_up, w_down)


def add_bf16(*terms):
    total = terms[0].astype(jnp.float32)
    for term in terms[1:]:
        total = total + term.astype(jnp.float32)
    return total.astype(jnp.bfloat16)


def body(
    stream,
    queries,
    attn_keys,
    attn_values,
    out_weight,
    norm_gain,
    expert_ids,
    combine,
    w_gate,
    w_up,
    w_down,
):
    n_ctx, n_exp = lax.axis_size("ctx"), lax.axis_size("exp")
    ctx_pos, exp_pos = lax.axis_index("ctx"), lax.axis_index("exp")
    tok_rows = stream.shape[0]
    chips = range(2, n_ctx, 2)

    kv = jnp.concatenate([attn_keys, attn_values], axis=1)
    near = jnp.concatenate([kv] + [swap(kv, "ctx", m) for m in chips], axis=0)
    far = swap(near, "ctx", 1)
    where = jnp.stack([ctx_pos, exp_pos]).astype(jnp.int32)
    partial = attend(where, queries, near, far, out_weight, n_exp, tok_rows)
    arrived = [partial[0]] + [swap(partial[k], "exp", k) for k in range(1, n_exp)]
    mixed, normed = add_and_norm(stream, norm_gain, arrived)

    planes = [normed] + [swap(normed, "exp", k) for k in range(1, n_exp)]
    groups = [[k] for k in range(min(2, n_exp))]
    if n_exp > 2:
        groups.append(list(range(2, n_exp)))
    returned = {}
    for group in groups:
        own = planes[group[0]] if len(group) == 1 else jnp.concatenate([planes[k] for k in group])
        lane = [own] + [swap(own, "ctx", m) for m in chips]
        other = [swap(piece, "ctx", 1) for piece in lane]
        keep, send = expert_rows(lane + other, w_gate, w_up, w_down)
        got = swap(send, "ctx", 1)
        rows = own.shape[0]
        pieces = [
            add_bf16(keep[i * rows : (i + 1) * rows], got[i * rows : (i + 1) * rows])
            for i in range(len(lane))
        ]
        total = add_bf16(pieces[0], *[swap(p, "ctx", m) for p, m in zip(pieces[1:], chips)])
        for i, k in enumerate(group):
            piece = total[i * tok_rows : (i + 1) * tok_rows]
            returned[k] = swap(piece, "exp", k) if k else piece
    update = jnp.zeros(mixed.shape, jnp.float32)
    for k in range(n_exp):
        share = jnp.sum(jnp.where(expert_ids == (exp_pos ^ k), combine, 0.0), axis=1, keepdims=True)
        update = update + share * returned[k].astype(jnp.float32)
    return (mixed + update).astype(jnp.bfloat16)


def solution(mesh):
    in_specs = (
        P(("ctx", "exp"), None),
        P("ctx", "exp"),
        P("ctx", "exp"),
        P("ctx", "exp"),
        P("exp", None),
        P(),
        P(("ctx", "exp"), None),
        P(("ctx", "exp"), None),
        P("exp", None, "ctx"),
        P("exp", None, "ctx"),
        P("exp", "ctx", None),
    )
    out_specs = P(("ctx", "exp"), None)
    return jax.shard_map(body, mesh=mesh, in_specs=in_specs, out_specs=out_specs, check_vma=False)
```

```python
import functools
import math

import jax
import jax.numpy as jnp
from jax import lax
from jax.experimental import pallas as pl
from jax.experimental.pallas import tpu as pltpu
from jax.sharding import PartitionSpec as P

HEAD_DIM = 128
TOP = 2
GROUP = 4
MASKED = -1e30
MIB = 1 << 20
UP_SLOTS = 4
DOWN_SLOTS = 4
DOWN_TILE = 1024
LAG = 2
CUT = 1


def swap(value, axis, mask):
    count = lax.axis_size(axis)
    return lax.ppermute(value, axis, [(i, i ^ mask) for i in range(count)])


def attend_kernel(
    n_exp, tok_rows, where_ref, q_ref, near_ref, far_ref, weight_hbm, *rest
):
    outs, (att_ref, sorted_ref, weight_ref, weight_sem) = rest[:n_exp], rest[n_exp:]
    fetch = pltpu.make_async_copy(weight_hbm, weight_ref, weight_sem)
    fetch.start()
    span = q_ref.shape[0]
    kv_width = near_ref.shape[1] // 2
    kv_heads = kv_width // HEAD_DIM
    ctx_pos, exp_pos = where_ref[0], where_ref[1]
    n_keys = near_ref.shape[0]
    query_pos = ctx_pos * span + lax.broadcasted_iota(jnp.int32, (span, n_keys), 0)
    column = lax.broadcasted_iota(jnp.int32, (span, n_keys), 1)
    block, within = column // span, column % span
    masks = []
    for core in range(2):
        key_pos = (ctx_pos ^ (2 * block + core)) * span + within
        masks.append(query_pos >= key_pos)
    scale = 1.0 / math.sqrt(HEAD_DIM)
    for g in range(kv_heads):
        keys = slice(g * HEAD_DIM, (g + 1) * HEAD_DIM)
        values = slice(kv_width + g * HEAD_DIM, kv_width + (g + 1) * HEAD_DIM)
        for r in range(GROUP):
            h = g * GROUP + r
            q = q_ref[:, h * HEAD_DIM : (h + 1) * HEAD_DIM]
            scores = []
            for ref, mask in zip((near_ref, far_ref), masks):
                s = lax.dot_general(
                    q, ref[:, keys], (((1,), (1,)), ((), ())), preferred_element_type=jnp.float32
                )
                scores.append(jnp.where(mask, s * scale, MASKED))
            top = jnp.maximum(
                jnp.max(scores[0], axis=1, keepdims=True), jnp.max(scores[1], axis=1, keepdims=True)
            )
            total = jnp.zeros((span, 1), jnp.float32)
            acc = jnp.zeros((span, HEAD_DIM), jnp.float32)
            for ref, s in zip((near_ref, far_ref), scores):
                w = jnp.exp(s - top)
                total = total + jnp.sum(w, axis=1, keepdims=True)
                acc = acc + jnp.dot(
                    w.astype(jnp.bfloat16), ref[:, values], preferred_element_type=jnp.float32
                )
            att_ref[:, h * HEAD_DIM : (h + 1) * HEAD_DIM] = (acc / total).astype(jnp.bfloat16)
    for k in range(n_exp):
        first = pl.multiple_of((exp_pos ^ k) * tok_rows, tok_rows)
        sorted_ref[k * tok_rows : (k + 1) * tok_rows, :] = att_ref[pl.ds(first, tok_rows), :]
    fetch.wait()
    model_dim = weight_ref.shape[1]
    tile = min(1024, model_dim)
    for lo in range(0, model_dim, tile):
        part = jnp.dot(
            sorted_ref[...], weight_ref[:, lo : lo + tile], preferred_element_type=jnp.float32
        ).astype(jnp.bfloat16)
        for k in range(n_exp):
            outs[k][:, lo : lo + tile] = part[k * tok_rows : (k + 1) * tok_rows]


def attend(where, queries, near, far, out_weight, n_exp, tok_rows):
    span = queries.shape[0]
    model_dim = out_weight.shape[1]
    vmem = pl.BlockSpec(memory_space=pltpu.VMEM)
    return pl.pallas_call(
        functools.partial(attend_kernel, n_exp, tok_rows),
        out_shape=[jax.ShapeDtypeStruct((tok_rows, model_dim), jnp.bfloat16)] * n_exp,
        in_specs=[
            pl.BlockSpec(memory_space=pltpu.SMEM),
            vmem,
            vmem,
            vmem,
            pl.BlockSpec(memory_space=pltpu.HBM),
        ],
        out_specs=[vmem] * n_exp,
        scratch_shapes=[
            pltpu.VMEM(queries.shape, jnp.bfloat16),
            pltpu.VMEM(queries.shape, jnp.bfloat16),
            pltpu.VMEM(out_weight.shape, jnp.bfloat16),
            pltpu.SemaphoreType.DMA(()),
        ],
        compiler_params=pltpu.CompilerParams(vmem_limit_bytes=24 * MIB),
        cost_estimate=pl.CostEstimate(
            flops=8 * 1000 * 1000 * 1000, bytes_accessed=12 * MIB, transcendentals=MIB
        ),
        name="attend",
    )(where, queries, near, far, out_weight)


def norm_kernel(stream_ref, gain_ref, *rest):
    parts, (mixed_ref, normed_ref) = rest[:-2], rest[-2:]
    mixed = stream_ref[...].astype(jnp.float32)
    update = parts[0][...].astype(jnp.float32)
    for part in parts[1:]:
        update = update + part[...].astype(jnp.float32)
    mixed = mixed + update
    mixed_ref[...] = mixed
    mean_square = jnp.mean(mixed * mixed, axis=-1, keepdims=True)
    normed_ref[...] = (mixed * lax.rsqrt(mean_square + 1e-05) * gain_ref[...]).astype(jnp.bfloat16)


def add_and_norm(stream, norm_gain, parts):
    vmem = pl.BlockSpec(memory_space=pltpu.VMEM)
    return pl.pallas_call(
        norm_kernel,
        out_shape=[
            jax.ShapeDtypeStruct(stream.shape, jnp.float32),
            jax.ShapeDtypeStruct(stream.shape, jnp.bfloat16),
        ],
        in_specs=[vmem] * (2 + len(parts)),
        out_specs=[vmem] * 2,
        compiler_params=pltpu.CompilerParams(vmem_limit_bytes=4 * MIB),
        cost_estimate=pl.CostEstimate(
            flops=6 * stream.size, bytes_accessed=20 * stream.size, transcendentals=0
        ),
        name="add_and_norm",
    )(stream, norm_gain.reshape(1, -1), *parts)


def expert_kernel(n_parts, n_after, *refs):
    parts, refs = refs[:n_parts], refs[n_parts + n_after :]
    gate_hbm, up_hbm, down_hbm, keep_ref, *sends = refs[:-8]
    rows_ref, hidden_ref, gate_ref, up_ref, down_ref, part_sems, up_sems, down_sems = refs[-8:]
    rows = parts[0].shape[0]
    model_dim, hidden_dim = gate_hbm.shape[1:]
    up_slots, tile = gate_ref.shape[0], gate_ref.shape[2]
    down_slots, down_tile = down_ref.shape[0], down_ref.shape[2]
    n_up, n_down = hidden_dim // tile, model_dim // down_tile

    def up_fetches(j):
        slot, units = j % up_slots, pl.ds(j * tile, tile)
        return [
            pltpu.make_async_copy(
                gate_hbm.at[0, :, units], gate_ref.at[slot], up_sems.at[0, slot]
            ),
            pltpu.make_async_copy(up_hbm.at[0, :, units], up_ref.at[slot], up_sems.at[1, slot]),
        ]

    def down_fetch(j):
        slot = j % down_slots
        return pltpu.make_async_copy(
            down_hbm.at[0, :, pl.ds(j * down_tile, down_tile)],
            down_ref.at[slot],
            down_sems.at[slot],
        )

    fetches = [
        pltpu.make_async_copy(part, rows_ref.at[pl.ds(i * rows, rows)], part_sems.at[i])
        for i, part in enumerate(parts)
    ]
    for fetch in fetches:
        fetch.start()
    for j in range(min(up_slots, n_up)):
        for fetch in up_fetches(j):
            fetch.start()
    for fetch in fetches:
        fetch.wait()
    ahead = 0
    for j in range(n_up):
        slot = j % up_slots
        for fetch in up_fetches(j):
            fetch.wait()
        gate = jnp.dot(rows_ref[...], gate_ref[slot], preferred_element_type=jnp.float32)
        up = jnp.dot(rows_ref[...], up_ref[slot], preferred_element_type=jnp.float32)
        hidden = (gate / (1.0 + jnp.exp(-gate)) * up).astype(jnp.bfloat16)
        hidden_ref[:, j * tile : (j + 1) * tile] = hidden
        if j + up_slots < n_up:
            for fetch in up_fetches(j + up_slots):
                fetch.start()
        elif ahead < min(down_slots, n_down):
            down_fetch(ahead).start()
            ahead += 1
    while ahead < min(down_slots, n_down):
        down_fetch(ahead).start()
        ahead += 1
    half = keep_ref.shape[0]
    for j in range(n_down):
        slot, columns = j % down_slots, slice(j * down_tile, (j + 1) * down_tile)
        down_fetch(j).wait()
        result = jnp.dot(
            hidden_ref[...], down_ref[slot], preferred_element_type=jnp.float32
        ).astype(jnp.bfloat16)
        if j + down_slots < n_down:
            down_fetch(j + down_slots).start()
        keep_ref[:, columns] = result[:half]
        cut = half // len(sends)
        for i, send_ref in enumerate(sends):
            send_ref[:, columns] = result[half + i * cut : half + (i + 1) * cut]


def expert_rows(parts, w_gate, w_up, w_down, after):
    n_parts, rows = len(parts), parts[0].shape[0]
    total = n_parts * rows
    _, model_dim, hidden_dim = w_gate.shape
    tile = 256 if hidden_dim % 256 == 0 else 128
    half = jax.ShapeDtypeStruct((total // 2, model_dim), jnp.bfloat16)
    n_send = CUT * n_parts // 2
    cut = jax.ShapeDtypeStruct((total // 2 // n_send, model_dim), jnp.bfloat16)
    vmem = pl.BlockSpec(memory_space=pltpu.VMEM)
    anywhere = pl.BlockSpec(memory_space=pl.ANY)
    keep, *send = pl.pallas_call(
        functools.partial(expert_kernel, n_parts, len(after)),
        out_shape=[half] + [cut] * n_send,
        in_specs=[anywhere] * (n_parts + len(after))
        + [pl.BlockSpec(memory_space=pltpu.HBM)] * 3,
        out_specs=[vmem] * (1 + n_send),
        scratch_shapes=[
            pltpu.VMEM((total, model_dim), jnp.bfloat16),
            pltpu.VMEM((total, hidden_dim), jnp.bfloat16),
            pltpu.VMEM((UP_SLOTS, model_dim, tile), jnp.bfloat16),
            pltpu.VMEM((UP_SLOTS, model_dim, tile), jnp.bfloat16),
            pltpu.VMEM((DOWN_SLOTS, hidden_dim, DOWN_TILE), jnp.bfloat16),
            pltpu.SemaphoreType.DMA((n_parts,)),
            pltpu.SemaphoreType.DMA((2, UP_SLOTS)),
            pltpu.SemaphoreType.DMA((DOWN_SLOTS,)),
        ],
        compiler_params=pltpu.CompilerParams(vmem_limit_bytes=48 * MIB),
        cost_estimate=pl.CostEstimate(
            flops=6 * total * model_dim * hidden_dim,
            bytes_accessed=2 * model_dim * hidden_dim,
            transcendentals=total * hidden_dim,
        ),
        name="expert_rows",
    )(*parts, *after, w_gate, w_up, w_down)
    return keep, send


def add_bf16(*terms):
    total = terms[0].astype(jnp.float32)
    for term in terms[1:]:
        total = total + term.astype(jnp.float32)
    return total.astype(jnp.bfloat16)


def body(
    stream,
    queries,
    attn_keys,
    attn_values,
    out_weight,
    norm_gain,
    expert_ids,
    combine,
    w_gate,
    w_up,
    w_down,
):
    n_ctx, n_exp = lax.axis_size("ctx"), lax.axis_size("exp")
    ctx_pos, exp_pos = lax.axis_index("ctx"), lax.axis_index("exp")
    tok_rows = stream.shape[0]
    chips = range(2, n_ctx, 2)

    kv = jnp.concatenate([attn_keys, attn_values], axis=1)
    near = jnp.concatenate([kv] + [swap(kv, "ctx", m) for m in chips], axis=0)
    far = swap(near, "ctx", 1)
    where = jnp.stack([ctx_pos, exp_pos]).astype(jnp.int32)
    partial = attend(where, queries, near, far, out_weight, n_exp, tok_rows)
    arrived = [partial[0]] + [swap(partial[k], "exp", k) for k in range(1, n_exp)]
    mixed, normed = add_and_norm(stream, norm_gain, arrived)

    def spread(rows):
        return [rows] + [swap(rows, "ctx", m) for m in chips]

    def across(lane):
        return [swap(rows, "exp", 1) for rows in lane]

    evens = list(range(0, n_exp, 2))
    order = [0] + [k + i for k in evens[1:] for i in (0, 1)] + [1]
    planes = {k: swap(normed, "exp", k) if k else normed for k in evens}
    lanes = {0: spread(normed)}
    pieces, totals, returned = {}, {}, {}

    def sum_plane(k):
        arrivals = [swap(p, "ctx", m) for p, m in zip(pieces[k][1:], chips)]
        totals[k] = add_bf16(pieces[k][0], *arrivals)
        returned[k] = swap(totals[k], "exp", k) if k else totals[k]

    for step, k in enumerate(order):
        if k % 2 == 0:
            lanes[k + 1] = across(lanes[k])
        other = [swap(rows, "ctx", 1) for rows in lanes[k]]
        after = []
        if step + 1 < n_exp and order[step + 1] % 2 == 0:
            following = order[step + 1]
            lanes[following] = spread(planes[following])
            after = after + [planes[following]]
        if step >= LAG:
            after = after + pieces[order[step - LAG]]
        if step >= LAG + 1:
            sum_plane(order[step - LAG - 1])
            after = after + [totals[order[step - LAG - 1]]]
        keep, send = expert_rows(lanes[k] + other, w_gate, w_up, w_down, after)
        got = [swap(part, "ctx", 1) for part in send]
        cuts = len(got) // len(lanes[k])
        pieces[k] = []
        for i in range(len(lanes[k])):
            mine = keep[i * tok_rows : (i + 1) * tok_rows]
            theirs = got[i * cuts : (i + 1) * cuts]
            theirs = jnp.concatenate(theirs) if cuts > 1 else theirs[0]
            pieces[k].append(add_bf16(mine, theirs))
    for k in order:
        if k not in totals:
            sum_plane(k)
    update = jnp.zeros(mixed.shape, jnp.float32)
    for k in range(n_exp):
        share = jnp.sum(jnp.where(expert_ids == (exp_pos ^ k), combine, 0.0), axis=1, keepdims=True)
        update = update + share * returned[k].astype(jnp.float32)
    return (mixed + update).astype(jnp.bfloat16)


def solution(mesh):
    in_specs = (
        P(("ctx", "exp"), None),
        P("ctx", "exp"),
        P("ctx", "exp"),
        P("ctx", "exp"),
        P("exp", None),
        P(),
        P(("ctx", "exp"), None),
        P(("ctx", "exp"), None),
        P("exp", None, "ctx"),
        P("exp", None, "ctx"),
        P("exp", "ctx", None),
    )
    out_specs = P(("ctx", "exp"), None)
    return jax.shard_map(body, mesh=mesh, in_specs=in_specs, out_specs=out_specs, check_vma=False)
```

```python
import functools
import math

import jax
import jax.numpy as jnp
from jax import lax
from jax.experimental import pallas as pl
from jax.experimental.pallas import tpu as pltpu
from jax.sharding import PartitionSpec as P

HEAD_DIM = 128
TOP = 2
GROUP = 4
MASKED = -1e30
MIB = 1 << 20
UP_SLOTS = 3
DOWN_SLOTS = 3
DOWN_TILE = 1024


def swap(value, axis, mask):
    count = lax.axis_size(axis)
    return lax.ppermute(value, axis, [(i, i ^ mask) for i in range(count)])


def in_hbm(*arrays):
    return [pltpu.with_memory_space_constraint(a, pltpu.HBM) for a in arrays]


def attend_kernel(
    n_exp, tok_rows, where_ref, q_ref, near_ref, far_ref, weight_hbm, *rest
):
    outs, (att_ref, sorted_ref, weight_ref, weight_sem) = rest[:n_exp], rest[n_exp:]
    fetch = pltpu.make_async_copy(weight_hbm, weight_ref, weight_sem)
    fetch.start()
    span = q_ref.shape[0]
    kv_width = near_ref.shape[1] // 2
    kv_heads = kv_width // HEAD_DIM
    ctx_pos, exp_pos = where_ref[0], where_ref[1]
    n_keys = near_ref.shape[0]
    query_pos = ctx_pos * span + lax.broadcasted_iota(jnp.int32, (span, n_keys), 0)
    column = lax.broadcasted_iota(jnp.int32, (span, n_keys), 1)
    block, within = column // span, column % span
    masks = []
    for core in range(2):
        key_pos = (ctx_pos ^ (2 * block + core)) * span + within
        masks.append(query_pos >= key_pos)
    scale = 1.0 / math.sqrt(HEAD_DIM)
    for g in range(kv_heads):
        keys = slice(g * HEAD_DIM, (g + 1) * HEAD_DIM)
        values = slice(kv_width + g * HEAD_DIM, kv_width + (g + 1) * HEAD_DIM)
        for r in range(GROUP):
            h = g * GROUP + r
            q = q_ref[:, h * HEAD_DIM : (h + 1) * HEAD_DIM]
            scores = []
            for ref, mask in zip((near_ref, far_ref), masks):
                s = lax.dot_general(
                    q, ref[:, keys], (((1,), (1,)), ((), ())), preferred_element_type=jnp.float32
                )
                scores.append(jnp.where(mask, s * scale, MASKED))
            top = jnp.maximum(
                jnp.max(scores[0], axis=1, keepdims=True), jnp.max(scores[1], axis=1, keepdims=True)
            )
            total = jnp.zeros((span, 1), jnp.float32)
            acc = jnp.zeros((span, HEAD_DIM), jnp.float32)
            for ref, s in zip((near_ref, far_ref), scores):
                w = jnp.exp(s - top)
                total = total + jnp.sum(w, axis=1, keepdims=True)
                acc = acc + jnp.dot(
                    w.astype(jnp.bfloat16), ref[:, values], preferred_element_type=jnp.float32
                )
            att_ref[:, h * HEAD_DIM : (h + 1) * HEAD_DIM] = (acc / total).astype(jnp.bfloat16)
    for k in range(n_exp):
        first = pl.multiple_of((exp_pos ^ k) * tok_rows, tok_rows)
        sorted_ref[k * tok_rows : (k + 1) * tok_rows, :] = att_ref[pl.ds(first, tok_rows), :]
    fetch.wait()
    model_dim = weight_ref.shape[1]
    tile = min(1024, model_dim)
    for lo in range(0, model_dim, tile):
        part = jnp.dot(
            sorted_ref[...], weight_ref[:, lo : lo + tile], preferred_element_type=jnp.float32
        ).astype(jnp.bfloat16)
        for k in range(n_exp):
            outs[k][:, lo : lo + tile] = part[k * tok_rows : (k + 1) * tok_rows]


def attend(where, queries, near, far, out_weight, n_exp, tok_rows):
    span = queries.shape[0]
    model_dim = out_weight.shape[1]
    vmem = pl.BlockSpec(memory_space=pltpu.VMEM)
    return pl.pallas_call(
        functools.partial(attend_kernel, n_exp, tok_rows),
        out_shape=[jax.ShapeDtypeStruct((tok_rows, model_dim), jnp.bfloat16)] * n_exp,
        in_specs=[
            pl.BlockSpec(memory_space=pltpu.SMEM),
            vmem,
            vmem,
            vmem,
            pl.BlockSpec(memory_space=pltpu.HBM),
        ],
        out_specs=[vmem] * n_exp,
        scratch_shapes=[
            pltpu.VMEM(queries.shape, jnp.bfloat16),
            pltpu.VMEM(queries.shape, jnp.bfloat16),
            pltpu.VMEM(out_weight.shape, jnp.bfloat16),
            pltpu.SemaphoreType.DMA(()),
        ],
        compiler_params=pltpu.CompilerParams(vmem_limit_bytes=24 * MIB),
        cost_estimate=pl.CostEstimate(
            flops=8 * 1000 * 1000 * 1000, bytes_accessed=12 * MIB, transcendentals=MIB
        ),
        name="attend",
    )(where, queries, near, far, *in_hbm(out_weight))


def norm_kernel(stream_ref, gain_ref, *rest):
    parts, (mixed_ref, normed_ref) = rest[:-2], rest[-2:]
    mixed = stream_ref[...].astype(jnp.float32)
    update = parts[0][...].astype(jnp.float32)
    for part in parts[1:]:
        update = update + part[...].astype(jnp.float32)
    mixed = mixed + update
    mixed_ref[...] = mixed
    mean_square = jnp.mean(mixed * mixed, axis=-1, keepdims=True)
    normed_ref[...] = (mixed * lax.rsqrt(mean_square + 1e-05) * gain_ref[...]).astype(jnp.bfloat16)


def add_and_norm(stream, norm_gain, parts):
    vmem = pl.BlockSpec(memory_space=pltpu.VMEM)
    return pl.pallas_call(
        norm_kernel,
        out_shape=[
            jax.ShapeDtypeStruct(stream.shape, jnp.float32),
            jax.ShapeDtypeStruct(stream.shape, jnp.bfloat16),
        ],
        in_specs=[vmem] * (2 + len(parts)),
        out_specs=[vmem] * 2,
        compiler_params=pltpu.CompilerParams(vmem_limit_bytes=4 * MIB),
        cost_estimate=pl.CostEstimate(
            flops=6 * stream.size, bytes_accessed=20 * stream.size, transcendentals=0
        ),
        name="add_and_norm",
    )(stream, norm_gain.reshape(1, -1), *parts)


def expert_kernel(n_parts, n_after, *refs):
    parts, refs = refs[:n_parts], refs[n_parts + n_after :]
    gate_hbm, up_hbm, down_hbm, keep_ref, send_ref = refs[:-8]
    rows_ref, hidden_ref, gate_ref, up_ref, down_ref, part_sems, up_sems, down_sems = refs[-8:]
    rows = rows_ref.shape[0] // n_parts
    model_dim, hidden_dim = gate_hbm.shape[1:]
    up_slots, tile = gate_ref.shape[0], gate_ref.shape[2]
    down_slots, down_tile = down_ref.shape[0], down_ref.shape[2]
    n_up, n_down = hidden_dim // tile, model_dim // down_tile

    def up_fetches(j):
        slot, units = j % up_slots, pl.ds(j * tile, tile)
        return [
            pltpu.make_async_copy(
                gate_hbm.at[0, :, units], gate_ref.at[slot], up_sems.at[0, slot]
            ),
            pltpu.make_async_copy(up_hbm.at[0, :, units], up_ref.at[slot], up_sems.at[1, slot]),
        ]

    def down_fetch(j):
        slot = j % down_slots
        return pltpu.make_async_copy(
            down_hbm.at[0, :, pl.ds(j * down_tile, down_tile)],
            down_ref.at[slot],
            down_sems.at[slot],
        )

    fetches = [
        pltpu.make_async_copy(
            part.at[pl.ds(0, rows)], rows_ref.at[pl.ds(i * rows, rows)], part_sems.at[i]
        )
        for i, part in enumerate(parts)
    ]
    for fetch in fetches:
        fetch.start()
    for j in range(min(up_slots, n_up)):
        for fetch in up_fetches(j):
            fetch.start()
    for fetch in fetches:
        fetch.wait()
    ahead = 0
    for j in range(n_up):
        slot = j % up_slots
        for fetch in up_fetches(j):
            fetch.wait()
        gate = jnp.dot(rows_ref[...], gate_ref[slot], preferred_element_type=jnp.float32)
        up = jnp.dot(rows_ref[...], up_ref[slot], preferred_element_type=jnp.float32)
        hidden = (gate / (1.0 + jnp.exp(-gate)) * up).astype(jnp.bfloat16)
        hidden_ref[:, j * tile : (j + 1) * tile] = hidden
        if j + up_slots < n_up:
            for fetch in up_fetches(j + up_slots):
                fetch.start()
        elif ahead < min(down_slots, n_down):
            down_fetch(ahead).start()
            ahead += 1
    while ahead < min(down_slots, n_down):
        down_fetch(ahead).start()
        ahead += 1
    half = keep_ref.shape[0]
    for j in range(n_down):
        slot, columns = j % down_slots, slice(j * down_tile, (j + 1) * down_tile)
        down_fetch(j).wait()
        result = jnp.dot(
            hidden_ref[...], down_ref[slot], preferred_element_type=jnp.float32
        ).astype(jnp.bfloat16)
        if j + down_slots < n_down:
            down_fetch(j + down_slots).start()
        keep_ref[:, columns] = result[:half]
        send_ref[:, columns] = result[half:]


def expert_rows(parts, rows, w_gate, w_up, w_down, after):
    n_parts, total = len(parts), len(parts) * rows
    _, model_dim, hidden_dim = w_gate.shape
    tile = 256 if hidden_dim % 256 == 0 else 128
    half = jax.ShapeDtypeStruct((total // 2, model_dim), jnp.bfloat16)
    vmem = pl.BlockSpec(memory_space=pltpu.VMEM)
    anywhere = pl.BlockSpec(memory_space=pl.ANY)
    return pl.pallas_call(
        functools.partial(expert_kernel, n_parts, len(after)),
        out_shape=[half, half],
        in_specs=[anywhere] * (n_parts + len(after))
        + [pl.BlockSpec(memory_space=pltpu.HBM)] * 3,
        out_specs=[vmem, vmem],
        scratch_shapes=[
            pltpu.VMEM((total, model_dim), jnp.bfloat16),
            pltpu.VMEM((total, hidden_dim), jnp.bfloat16),
            pltpu.VMEM((UP_SLOTS, model_dim, tile), jnp.bfloat16),
            pltpu.VMEM((UP_SLOTS, model_dim, tile), jnp.bfloat16),
            pltpu.VMEM((DOWN_SLOTS, hidden_dim, DOWN_TILE), jnp.bfloat16),
            pltpu.SemaphoreType.DMA((n_parts,)),
            pltpu.SemaphoreType.DMA((2, UP_SLOTS)),
            pltpu.SemaphoreType.DMA((DOWN_SLOTS,)),
        ],
        compiler_params=pltpu.CompilerParams(vmem_limit_bytes=32 * MIB),
        cost_estimate=pl.CostEstimate(
            flops=6 * total * model_dim * hidden_dim,
            bytes_accessed=2 * model_dim * hidden_dim,
            transcendentals=total * hidden_dim,
        ),
        name="expert_rows",
    )(*parts, *after, *in_hbm(w_gate, w_up, w_down))


def pack_kernel(n_parts, *refs):
    out, first = refs[-1], 0
    for part in refs[:n_parts]:
        out[first : first + part.shape[0], :] = part[...]
        first += part.shape[0]


def pack(parts, after):
    rows, model_dim = sum(part.shape[0] for part in parts), parts[0].shape[1]
    vmem, anywhere = pl.BlockSpec(memory_space=pltpu.VMEM), pl.BlockSpec(memory_space=pl.ANY)
    return pl.pallas_call(
        functools.partial(pack_kernel, len(parts)),
        out_shape=jax.ShapeDtypeStruct((rows, model_dim), jnp.bfloat16),
        in_specs=[vmem] * len(parts) + [anywhere] * len(after),
        out_specs=vmem,
        compiler_params=pltpu.CompilerParams(vmem_limit_bytes=2 * MIB),
        cost_estimate=pl.CostEstimate(
            flops=0, bytes_accessed=4 * rows * model_dim, transcendentals=0
        ),
        name="pack",
    )(*parts, *after)


def add_bf16(*terms):
    total = terms[0].astype(jnp.float32)
    for term in terms[1:]:
        total = total + term.astype(jnp.float32)
    return total.astype(jnp.bfloat16)


def body(
    stream,
    queries,
    attn_keys,
    attn_values,
    out_weight,
    norm_gain,
    expert_ids,
    combine,
    w_gate,
    w_up,
    w_down,
):
    n_ctx, n_exp = lax.axis_size("ctx"), lax.axis_size("exp")
    ctx_pos, exp_pos = lax.axis_index("ctx"), lax.axis_index("exp")
    tok_rows = stream.shape[0]
    chips = range(2, n_ctx, 2)

    kv = jnp.concatenate([attn_keys, attn_values], axis=1)
    near = jnp.concatenate([kv] + [swap(kv, "ctx", m) for m in chips], axis=0)
    far = swap(near, "ctx", 1)
    where = jnp.stack([ctx_pos, exp_pos]).astype(jnp.int32)
    partial = attend(where, queries, near, far, out_weight, n_exp, tok_rows)
    arrived = [partial[0]] + [swap(partial[k], "exp", k) for k in range(1, n_exp)]
    mixed, normed = add_and_norm(stream, norm_gain, arrived)

    n_lanes = 1 + len(chips)
    half = n_lanes * tok_rows
    evens = list(range(0, n_exp, 2))
    planes = {k: swap(normed, "exp", k) if k else normed for k in evens}
    spreads = {k: [planes[k]] + [swap(planes[k], "ctx", m) for m in chips] for k in evens}
    pieces, totals, returned = [], [], []

    def sum_core(keep, got, first):
        pieces.append(
            [
                add_bf16(keep[lo : lo + tok_rows], got[first + lo : first + lo + tok_rows])
                for lo in range(0, half, tok_rows)
            ]
        )

    def sum_plane(k):
        arrivals = [swap(p, "ctx", m) for p, m in zip(pieces[k][1:], chips)]
        totals.append(add_bf16(pieces[k][0], *arrivals))
        returned.append(swap(totals[k], "exp", k) if k else totals[k])

    lane = pack(spreads[0], [planes[2]] if n_exp > 2 else [])
    spreads[1] = [swap(lane, "exp", 1)]
    other = swap(lane, "ctx", 1)
    keep, send = expert_rows([lane, other], half, w_gate, w_up, w_down, [])
    for k in range(1, n_exp):
        gates = []
        if k + 1 < n_exp:
            if k % 2:
                spreads[k + 1] = [pack(spreads[k + 1], [keep])]
                spreads[k + 2] = [swap(spreads[k + 1][0], "exp", 1)]
                gates = gates + spreads[k + 1]
            else:
                gates = gates + spreads[k + 1]
        if k >= 2:
            sum_plane(k - 2)
            gates = gates + [totals[k - 2]]
        if k >= 3:
            gates = gates + [returned[k - 3]]
        lane = pack(spreads[k] + [send], gates)
        other = swap(lane, "ctx", 1)
        sum_core(keep, other, half)
        keep, send = expert_rows([lane, other], half, w_gate, w_up, w_down, [])
    gates = []
    if n_exp >= 2:
        sum_plane(n_exp - 2)
        gates = gates + [totals[n_exp - 2]]
    if n_exp >= 3:
        gates = gates + [returned[n_exp - 3]]
    sum_core(keep, swap(pack([send], gates), "ctx", 1), 0)
    for k in range(len(totals), n_exp):
        sum_plane(k)
    update = jnp.zeros(mixed.shape, jnp.float32)
    for k in range(n_exp):
        share = jnp.sum(jnp.where(expert_ids == (exp_pos ^ k), combine, 0.0), axis=1, keepdims=True)
        update = update + share * returned[k].astype(jnp.float32)
    return (mixed + update).astype(jnp.bfloat16)


def solution(mesh):
    in_specs = (
        P(("ctx", "exp"), None),
        P("ctx", "exp"),
        P("ctx", "exp"),
        P("ctx", "exp"),
        P("exp", None),
        P(),
        P(("ctx", "exp"), None),
        P(("ctx", "exp"), None),
        P("exp", None, "ctx"),
        P("exp", None, "ctx"),
        P("exp", "ctx", None),
    )
    out_specs = P(("ctx", "exp"), None)
    return jax.shard_map(body, mesh=mesh, in_specs=in_specs, out_specs=out_specs, check_vma=False)
```

```python
import functools
import math

import jax
import jax.numpy as jnp
from jax import lax
from jax.experimental import pallas as pl
from jax.experimental.pallas import tpu as pltpu
from jax.sharding import PartitionSpec as P

HEAD_DIM = 128
TOP = 2
GROUP = 4
MASKED = -1e30
MIB = 1 << 20
UP_SLOTS = 3
DOWN_SLOTS = 3
DOWN_TILE = 1024


def swap(value, axis, mask):
    count = lax.axis_size(axis)
    return lax.ppermute(value, axis, [(i, i ^ mask) for i in range(count)])


def in_hbm(*arrays):
    return [pltpu.with_memory_space_constraint(a, pltpu.HBM) for a in arrays]


def attend_kernel(
    n_exp, tok_rows, where_ref, q_ref, near_ref, far_ref, weight_hbm, *rest
):
    outs, (att_ref, sorted_ref, weight_ref, weight_sem) = rest[:n_exp], rest[n_exp:]
    tile = weight_ref.shape[1] // weight_sem.shape[0]
    tiles = [slice(i * tile, (i + 1) * tile) for i in range(weight_sem.shape[0])]
    fetches = [
        pltpu.make_async_copy(weight_hbm.at[:, t], weight_ref.at[:, t], weight_sem.at[i])
        for i, t in enumerate(tiles)
    ]
    for fetch in fetches:
        fetch.start()
    span = q_ref.shape[0]
    kv_width = near_ref.shape[1] // 2
    kv_heads = kv_width // HEAD_DIM
    ctx_pos, exp_pos = where_ref[0], where_ref[1]
    n_keys = near_ref.shape[0]
    query_pos = ctx_pos * span + lax.broadcasted_iota(jnp.int32, (span, n_keys), 0)
    column = lax.broadcasted_iota(jnp.int32, (span, n_keys), 1)
    block, within = column // span, column % span
    masks = []
    for core in range(2):
        key_pos = (ctx_pos ^ (2 * block + core)) * span + within
        masks.append(query_pos >= key_pos)
    scale = 1.0 / math.sqrt(HEAD_DIM)
    for g in range(kv_heads):
        keys = slice(g * HEAD_DIM, (g + 1) * HEAD_DIM)
        values = slice(kv_width + g * HEAD_DIM, kv_width + (g + 1) * HEAD_DIM)
        for r in range(GROUP):
            h = g * GROUP + r
            q = q_ref[:, h * HEAD_DIM : (h + 1) * HEAD_DIM]
            scores = []
            for ref, mask in zip((near_ref, far_ref), masks):
                s = lax.dot_general(
                    q, ref[:, keys], (((1,), (1,)), ((), ())), preferred_element_type=jnp.float32
                )
                scores.append(jnp.where(mask, s * scale, MASKED))
            top = jnp.maximum(
                jnp.max(scores[0], axis=1, keepdims=True), jnp.max(scores[1], axis=1, keepdims=True)
            )
            total = jnp.zeros((span, 1), jnp.float32)
            acc = jnp.zeros((span, HEAD_DIM), jnp.float32)
            for ref, s in zip((near_ref, far_ref), scores):
                w = jnp.exp(s - top)
                total = total + jnp.sum(w, axis=1, keepdims=True)
                acc = acc + jnp.dot(
                    w.astype(jnp.bfloat16), ref[:, values], preferred_element_type=jnp.float32
                )
            att_ref[:, h * HEAD_DIM : (h + 1) * HEAD_DIM] = (acc / total).astype(jnp.bfloat16)
    for k in range(n_exp):
        first = pl.multiple_of((exp_pos ^ k) * tok_rows, tok_rows)
        sorted_ref[k * tok_rows : (k + 1) * tok_rows, :] = att_ref[pl.ds(first, tok_rows), :]
    for fetch, t in zip(fetches, tiles):
        fetch.wait()
        part = jnp.dot(
            sorted_ref[...], weight_ref[:, t], preferred_element_type=jnp.float32
        ).astype(jnp.bfloat16)
        for k in range(n_exp):
            outs[k][:, t] = part[k * tok_rows : (k + 1) * tok_rows]


def attend(where, queries, near, far, out_weight, n_exp, tok_rows):
    span = queries.shape[0]
    model_dim = out_weight.shape[1]
    vmem = pl.BlockSpec(memory_space=pltpu.VMEM)
    return pl.pallas_call(
        functools.partial(attend_kernel, n_exp, tok_rows),
        out_shape=[jax.ShapeDtypeStruct((tok_rows, model_dim), jnp.bfloat16)] * n_exp,
        in_specs=[
            pl.BlockSpec(memory_space=pltpu.SMEM),
            vmem,
            vmem,
            vmem,
            pl.BlockSpec(memory_space=pltpu.HBM),
        ],
        out_specs=[vmem] * n_exp,
        scratch_shapes=[
            pltpu.VMEM(queries.shape, jnp.bfloat16),
            pltpu.VMEM(queries.shape, jnp.bfloat16),
            pltpu.VMEM(out_weight.shape, jnp.bfloat16),
            pltpu.SemaphoreType.DMA((out_weight.shape[1] // 512,)),
        ],
        compiler_params=pltpu.CompilerParams(vmem_limit_bytes=24 * MIB),
        cost_estimate=pl.CostEstimate(
            flops=8 * 1000 * 1000 * 1000, bytes_accessed=12 * MIB, transcendentals=MIB
        ),
        name="attend",
    )(where, queries, near, far, *in_hbm(out_weight))


def norm_kernel(stream_ref, gain_ref, *rest):
    parts, (mixed_ref, normed_ref) = rest[:-2], rest[-2:]
    mixed = stream_ref[...].astype(jnp.float32)
    update = parts[0][...].astype(jnp.float32)
    for part in parts[1:]:
        update = update + part[...].astype(jnp.float32)
    mixed = mixed + update
    mixed_ref[...] = mixed
    mean_square = jnp.mean(mixed * mixed, axis=-1, keepdims=True)
    normed_ref[...] = (mixed * lax.rsqrt(mean_square + 1e-05) * gain_ref[...]).astype(jnp.bfloat16)


def add_and_norm(stream, norm_gain, parts):
    vmem = pl.BlockSpec(memory_space=pltpu.VMEM)
    return pl.pallas_call(
        norm_kernel,
        out_shape=[
            jax.ShapeDtypeStruct(stream.shape, jnp.float32),
            jax.ShapeDtypeStruct(stream.shape, jnp.bfloat16),
        ],
        in_specs=[vmem] * (2 + len(parts)),
        out_specs=[vmem] * 2,
        compiler_params=pltpu.CompilerParams(vmem_limit_bytes=4 * MIB),
        cost_estimate=pl.CostEstimate(
            flops=6 * stream.size, bytes_accessed=20 * stream.size, transcendentals=0
        ),
        name="add_and_norm",
    )(stream, norm_gain.reshape(1, -1), *parts)


def expert_kernel(n_parts, n_after, *refs):
    parts, refs = refs[:n_parts], refs[n_parts + n_after :]
    gate_hbm, up_hbm, down_hbm, keep_ref, send_ref = refs[:-8]
    rows_ref, hidden_ref, gate_ref, up_ref, down_ref, part_sems, up_sems, down_sems = refs[-8:]
    rows = rows_ref.shape[0] // n_parts
    model_dim, hidden_dim = gate_hbm.shape[1:]
    up_slots, tile = gate_ref.shape[0], gate_ref.shape[2]
    down_slots, down_tile = down_ref.shape[0], down_ref.shape[2]
    n_up, n_down = hidden_dim // tile, model_dim // down_tile

    def up_fetches(j):
        slot, units = j % up_slots, pl.ds(j * tile, tile)
        return [
            pltpu.make_async_copy(
                gate_hbm.at[0, :, units], gate_ref.at[slot], up_sems.at[0, slot]
            ),
            pltpu.make_async_copy(up_hbm.at[0, :, units], up_ref.at[slot], up_sems.at[1, slot]),
        ]

    def down_fetch(j):
        slot = j % down_slots
        return pltpu.make_async_copy(
            down_hbm.at[0, :, pl.ds(j * down_tile, down_tile)],
            down_ref.at[slot],
            down_sems.at[slot],
        )

    fetches = [
        pltpu.make_async_copy(
            part.at[pl.ds(0, rows)], rows_ref.at[pl.ds(i * rows, rows)], part_sems.at[i]
        )
        for i, part in enumerate(parts)
    ]
    for fetch in fetches:
        fetch.start()
    for j in range(min(up_slots, n_up)):
        for fetch in up_fetches(j):
            fetch.start()
    for fetch in fetches:
        fetch.wait()
    ahead = 0
    for j in range(n_up):
        slot = j % up_slots
        for fetch in up_fetches(j):
            fetch.wait()
        gate = jnp.dot(rows_ref[...], gate_ref[slot], preferred_element_type=jnp.float32)
        up = jnp.dot(rows_ref[...], up_ref[slot], preferred_element_type=jnp.float32)
        hidden = (gate / (1.0 + jnp.exp(-gate)) * up).astype(jnp.bfloat16)
        hidden_ref[:, j * tile : (j + 1) * tile] = hidden
        if j + up_slots < n_up:
            for fetch in up_fetches(j + up_slots):
                fetch.start()
        elif ahead < min(down_slots, n_down):
            down_fetch(ahead).start()
            ahead += 1
    while ahead < min(down_slots, n_down):
        down_fetch(ahead).start()
        ahead += 1
    half = keep_ref.shape[0]
    for j in range(n_down):
        slot, columns = j % down_slots, slice(j * down_tile, (j + 1) * down_tile)
        down_fetch(j).wait()
        result = jnp.dot(
            hidden_ref[...], down_ref[slot], preferred_element_type=jnp.float32
        ).astype(jnp.bfloat16)
        if j + down_slots < n_down:
            down_fetch(j + down_slots).start()
        keep_ref[:, columns] = result[:half]
        send_ref[:, columns] = result[half:]


def expert_rows(parts, rows, w_gate, w_up, w_down, after):
    n_parts, total = len(parts), len(parts) * rows
    _, model_dim, hidden_dim = w_gate.shape
    tile = 256 if hidden_dim % 256 == 0 else 128
    half = jax.ShapeDtypeStruct((total // 2, model_dim), jnp.bfloat16)
    vmem = pl.BlockSpec(memory_space=pltpu.VMEM)
    anywhere = pl.BlockSpec(memory_space=pl.ANY)
    return pl.pallas_call(
        functools.partial(expert_kernel, n_parts, len(after)),
        out_shape=[half, half],
        in_specs=[anywhere] * (n_parts + len(after))
        + [pl.BlockSpec(memory_space=pltpu.HBM)] * 3,
        out_specs=[vmem, vmem],
        scratch_shapes=[
            pltpu.VMEM((total, model_dim), jnp.bfloat16),
            pltpu.VMEM((total, hidden_dim), jnp.bfloat16),
            pltpu.VMEM((UP_SLOTS, model_dim, tile), jnp.bfloat16),
            pltpu.VMEM((UP_SLOTS, model_dim, tile), jnp.bfloat16),
            pltpu.VMEM((DOWN_SLOTS, hidden_dim, DOWN_TILE), jnp.bfloat16),
            pltpu.SemaphoreType.DMA((n_parts,)),
            pltpu.SemaphoreType.DMA((2, UP_SLOTS)),
            pltpu.SemaphoreType.DMA((DOWN_SLOTS,)),
        ],
        compiler_params=pltpu.CompilerParams(vmem_limit_bytes=32 * MIB),
        cost_estimate=pl.CostEstimate(
            flops=6 * total * model_dim * hidden_dim,
            bytes_accessed=2 * model_dim * hidden_dim,
            transcendentals=total * hidden_dim,
        ),
        name="expert_rows",
    )(*parts, *after, *in_hbm(w_gate, w_up, w_down))


def pack_kernel(n_parts, *refs):
    out, first = refs[-1], 0
    for part in refs[:n_parts]:
        out[first : first + part.shape[0], :] = part[...]
        first += part.shape[0]


def pack(parts, after):
    rows, model_dim = sum(part.shape[0] for part in parts), parts[0].shape[1]
    vmem, anywhere = pl.BlockSpec(memory_space=pltpu.VMEM), pl.BlockSpec(memory_space=pl.ANY)
    return pl.pallas_call(
        functools.partial(pack_kernel, len(parts)),
        out_shape=jax.ShapeDtypeStruct((rows, model_dim), jnp.bfloat16),
        in_specs=[vmem] * len(parts) + [anywhere] * len(after),
        out_specs=vmem,
        compiler_params=pltpu.CompilerParams(vmem_limit_bytes=2 * MIB),
        cost_estimate=pl.CostEstimate(
            flops=0, bytes_accessed=4 * rows * model_dim, transcendentals=0
        ),
        name="pack",
    )(*parts, *after)


def add_bf16(*terms):
    total = terms[0].astype(jnp.float32)
    for term in terms[1:]:
        total = total + term.astype(jnp.float32)
    return total.astype(jnp.bfloat16)


def body(
    stream,
    queries,
    attn_keys,
    attn_values,
    out_weight,
    norm_gain,
    expert_ids,
    combine,
    w_gate,
    w_up,
    w_down,
):
    n_ctx, n_exp = lax.axis_size("ctx"), lax.axis_size("exp")
    ctx_pos, exp_pos = lax.axis_index("ctx"), lax.axis_index("exp")
    tok_rows = stream.shape[0]
    chips = range(2, n_ctx, 2)

    kv = jnp.concatenate([attn_keys, attn_values], axis=1)
    near = jnp.concatenate([kv] + [swap(kv, "ctx", m) for m in chips], axis=0)
    far = swap(near, "ctx", 1)
    where = jnp.stack([ctx_pos, exp_pos]).astype(jnp.int32)
    partial = attend(where, queries, near, far, out_weight, n_exp, tok_rows)
    arrived = [partial[0]] + [swap(partial[k], "exp", k) for k in range(1, n_exp)]
    mixed, normed = add_and_norm(stream, norm_gain, arrived)

    n_lanes = 1 + len(chips)
    half = n_lanes * tok_rows
    evens = list(range(0, n_exp, 2))
    planes = {k: swap(normed, "exp", k) if k else normed for k in evens}
    spreads = {k: [planes[k]] + [swap(planes[k], "ctx", m) for m in chips] for k in evens}
    pieces, totals, returned = [], [], []

    def sum_core(keep, got, first):
        pieces.append(
            [
                add_bf16(keep[lo : lo + tok_rows], got[first + lo : first + lo + tok_rows])
                for lo in range(0, half, tok_rows)
            ]
        )

    def sum_plane(k):
        arrivals = [swap(p, "ctx", m) for p, m in zip(pieces[k][1:], chips)]
        totals.append(add_bf16(pieces[k][0], *arrivals))
        returned.append(swap(totals[k], "exp", k) if k else totals[k])

    beside = swap(normed, "exp", 1)
    lane = pack(spreads[0], [beside] + ([planes[2]] if n_exp > 2 else []))
    spreads[1] = [beside, swap(pack(spreads[0][1:], []), "exp", 1)]
    other = swap(lane, "ctx", 1)
    keep, send = expert_rows([lane, other], half, w_gate, w_up, w_down, [])
    others = None
    for k in range(1, n_exp):
        gates = []
        if k + 1 < n_exp:
            if k % 2:
                spreads[k + 1] = [pack(spreads[k + 1], [keep])]
                spreads[k + 2] = [swap(spreads[k + 1][0], "exp", 1)]
                gates = gates + spreads[k + 1]
            else:
                gates = gates + spreads[k + 1]
        if k >= 2:
            sum_plane(k - 2)
            gates = gates + [totals[k - 2]]
        if k >= 3:
            gates = gates + [returned[k - 3]]
        if others is None:
            lane = pack(spreads[k] + [send], gates)
            other = swap(lane, "ctx", 1)
            sum_core(keep, other, half)
        else:
            lane, other = spreads[k][0], others
            sum_core(keep, swap(pack([send], gates + [other]), "ctx", 1), 0)
        others = swap(spreads[k + 1][0], "ctx", 1) if k + 1 < n_exp and k % 2 else None
        keep, send = expert_rows([lane, other], half, w_gate, w_up, w_down, [])
    gates = []
    if n_exp >= 2:
        sum_plane(n_exp - 2)
        gates = gates + [totals[n_exp - 2]]
    if n_exp >= 3:
        gates = gates + [returned[n_exp - 3]]
    sum_core(keep, swap(pack([send], gates), "ctx", 1), 0)
    for k in range(len(totals), n_exp):
        sum_plane(k)
    update = jnp.zeros(mixed.shape, jnp.float32)
    for k in range(n_exp):
        share = jnp.sum(jnp.where(expert_ids == (exp_pos ^ k), combine, 0.0), axis=1, keepdims=True)
        update = update + share * returned[k].astype(jnp.float32)
    return (mixed + update).astype(jnp.bfloat16)


def solution(mesh):
    in_specs = (
        P(("ctx", "exp"), None),
        P("ctx", "exp"),
        P("ctx", "exp"),
        P("ctx", "exp"),
        P("exp", None),
        P(),
        P(("ctx", "exp"), None),
        P(("ctx", "exp"), None),
        P("exp", None, "ctx"),
        P("exp", None, "ctx"),
        P("exp", "ctx", None),
    )
    out_specs = P(("ctx", "exp"), None)
    return jax.shard_map(body, mesh=mesh, in_specs=in_specs, out_specs=out_specs, check_vma=False)
```
